128 devices in a mesh: gr: 16 (over z, y_lo, core), gc: 8 (over y_hi, x).
Axes of the slice: x: 4, y: 4 (y_hi: 2, y_lo: 2; y = y_hi * 2 + y_lo), z: 4, core: 2. Of those that a mesh axis runs over, the one named last changes fastest.
Arguments:
- features: bfloat16 [65536, 128], P(('gr', 'gc')), may hold values from -6 to 6
- weight: bfloat16 [128, 128], replicated, may hold values from -0.5 to 0.5
- cotangent: bfloat16 [65536, 128], P(('gr', 'gc')), may hold values from -6 to 6
- tiles: bfloat16 [16, 8, 736, 128, 128], P('gr', 'gc')
- tile_rows: int32 [16, 8, 736], P('gr', 'gc'), may hold values from 0 to 31
- tile_cols: int32 [16, 8, 736], P('gr', 'gc'), may hold values from 0 to 63
- tile_counts: int32 [16, 8], P('gr', 'gc'), may hold values from 184 to 736, as said below
Outputs:
- output: bfloat16 [65536, 128], P(('gr', 'gc'))
- grad_features: bfloat16 [65536, 128], P(('gr', 'gc'))
- grad_weight: float32 [128, 128], replicated
The draws below stay inside these ranges and needn't reach their ends.
Inputs may be any that keep to these rules, and one draw needn't show every extreme that they name: `tile_counts`: some grid block holds exactly 736 live slots. `tile_rows`: positions may repeat within a block. `tile_cols`: positions may repeat within a block.
All inputs are finite; a program needn't handle non-finite values.
Results may differ from the reference program's by a relative error of at most 0.0075.
Values may be sent and summed in bfloat16 or wider, within the bound.
No kernel may reach another device: no remote copies, remote signals or barrier semaphores. Data moves between devices by JAX's collectives and lax.ppermute only.
A program may use at most 128 MiB of HBM per device.

```python
import math
import jax
import jax.numpy as jnp
from jax import lax

F = 128
TILE = 128
ROWS_DEV = 512
MAXT = 736
NODES = 65536
ROW_TILES = 32
COL_TILES = 64
N_GR = 16
N_GC = 8


def draw_tile_counts(key, part):
    key = jax.random.fold_in(key, 11)
    key_divisor, key_busiest = jax.random.split(key)
    divisor = 1 + jax.random.randint(key_divisor, (N_GR, N_GC), 0, 4)
    counts = MAXT // divisor
    busiest = jax.random.randint(key_busiest, (), 0, N_GR * N_GC)
    flat_counts = counts.reshape(-1)
    flat_counts = jnp.where(jnp.arange(N_GR * N_GC) == busiest, MAXT, flat_counts)
    return flat_counts.reshape(N_GR, N_GC).astype(jnp.int32)


def draw_tiles(key, part):
    key = jax.random.fold_in(key, 23)
    key_values = jax.random.fold_in(key, 0)
    spread = (2.0 * ROWS_DEV / (MAXT * TILE * TILE)) ** 0.5
    tile_shape = (N_GR, N_GC, MAXT, TILE, TILE)
    values = jax.random.normal(key_values, tile_shape, jnp.float32) * spread
    return values.astype(jnp.bfloat16)


def touch_ends(array, key, low, largest):
    place = [jax.random.randint(jax.random.fold_in(key, axis), (), 0, length) for axis, length in enumerate(array.shape)]
    main_axis = array.shape.index(max(array.shape))
    next_to = place[:main_axis] + [(place[main_axis] + 1) % array.shape[main_axis]] + place[main_axis + 1:]
    return array.at[tuple(place)].set(low).at[tuple(next_to)].set(largest)


def block_levels(key, extent, cuts, least, top_value):
    gain, own = 1.0, jax.random.fold_in(key, 6)
    for dim, shards_of in cuts:
        heights = jnp.exp(jax.random.uniform(jax.random.fold_in(own, dim), (shards_of,), jnp.float32, least / len(cuts), top_value / len(cuts)))
        gain = gain * jnp.repeat(heights, extent[dim] // shards_of).reshape([-1 if axis == dim else 1 for axis in range(len(extent))])
    return gain


def noise(own_key, extent, width, bound, pieces=(), kind=jnp.bfloat16):
    drawn = width * jax.random.normal(own_key, extent, jnp.float32)
    if pieces:
        drawn = drawn * block_levels(own_key, extent, pieces, -0.22, 0.18)
    return jnp.clip(drawn, -bound, bound).astype(kind)


def setup_inputs(seed: int = 0) -> dict:
    arg_keys = jax.random.split(jax.random.key(seed), 8)
    features = noise(arg_keys[0], (NODES, F), 1.0, 6.0, ((0, 128),))
    weight = noise(arg_keys[1], (F, F), F ** -0.5, 0.5)
    cotangent = noise(arg_keys[2], (NODES, F), 1.0, 6.0, ((0, 128),))
    tiles = draw_tiles(jax.random.fold_in(arg_keys[7], 71), 0)
    tile_rows = touch_ends(jax.random.randint(arg_keys[4], (N_GR, N_GC, MAXT), 0, ROW_TILES), jax.random.fold_in(arg_keys[4], 1), 0, ROW_TILES - 1).astype(jnp.int32)
    tile_cols = touch_ends(jax.random.randint(arg_keys[5], (N_GR, N_GC, MAXT), 0, COL_TILES), jax.random.fold_in(arg_keys[5], 1), 0, COL_TILES - 1).astype(jnp.int32)
    tile_counts = draw_tile_counts(jax.random.fold_in(arg_keys[7], 71), 0)
    return {"features": features, "weight": weight, "cotangent": cotangent, "tiles": tiles, "tile_rows": tile_rows, "tile_cols": tile_cols, "tile_counts": tile_counts}


def gelu_pair(pre_act):
    coeff = 0.7978845608028654
    cubed = pre_act * pre_act * pre_act
    tanh_val = jnp.tanh(coeff * (pre_act + 0.044715 * cubed))
    gelu_value = 0.5 * pre_act * (1.0 + tanh_val)
    gelu_slope = 0.5 * (1.0 + tanh_val) + 0.5 * pre_act * (1.0 - tanh_val * tanh_val) * coeff * (1.0 + 3.0 * 0.044715 * pre_act * pre_act)
    return (gelu_value, gelu_slope)

def tile_product(tile_block, source_ids, target_ids, tile_count, table, out_tiles, transposed):
    slot_index = jnp.arange(MAXT, dtype=jnp.int32)
    picked = table[source_ids].astype(jnp.float32)
    block_wide = tile_block.astype(jnp.float32)
    if transposed:
        products = jnp.einsum('sab,saf->sbf', block_wide, picked)
    else:
        products = jnp.einsum('sab,sbf->saf', block_wide, picked)
    live_mask = (slot_index < tile_count).astype(jnp.float32)
    products = products * live_mask[:, None, None]
    return jnp.zeros((out_tiles, TILE, F), jnp.float32).at[target_ids].add(products)

def reference(features, weight, cotangent, tiles, tile_rows, tile_cols, tile_counts):
    projected = jnp.dot(features, weight, preferred_element_type=jnp.float32).astype(jnp.bfloat16)
    proj_view = projected.reshape(N_GR, N_GC, ROWS_DEV, F)

    def row_block(grid_row):

        def add_column(totals, grid_col):
            column_set = lax.dynamic_index_in_dim(proj_view, grid_col, 1, keepdims=False).reshape(COL_TILES, TILE, F)
            term = tile_product(tiles[grid_row, grid_col], tile_cols[grid_row, grid_col], tile_rows[grid_row, grid_col], tile_counts[grid_row, grid_col], column_set, ROW_TILES, False)
            return (totals + term, None)
        start_rows = jnp.zeros((ROW_TILES, TILE, F), jnp.float32)
        totals, unused = lax.scan(add_column, start_rows, jnp.arange(N_GC, dtype=jnp.int32))
        return totals
    pre_act = lax.map(row_block, jnp.arange(N_GR, dtype=jnp.int32)).reshape(NODES, F)
    gelu_value, gelu_slope = gelu_pair(pre_act)
    output = gelu_value.astype(jnp.bfloat16)
    grad_pre = (cotangent.astype(jnp.float32) * gelu_slope).astype(jnp.bfloat16)
    grad_view = grad_pre.reshape(N_GR, ROW_TILES, TILE, F)

    def column_block(grid_col):

        def add_row(totals, grid_row):
            term = tile_product(tiles[grid_row, grid_col], tile_rows[grid_row, grid_col], tile_cols[grid_row, grid_col], tile_counts[grid_row, grid_col], grad_view[grid_row], COL_TILES, True)
            return (totals + term, None)
        start_cols = jnp.zeros((COL_TILES, TILE, F), jnp.float32)
        totals, unused = lax.scan(add_row, start_cols, jnp.arange(N_GR, dtype=jnp.int32))
        return totals
    column_sums = lax.map(column_block, jnp.arange(N_GC, dtype=jnp.int32))
    column_sums = column_sums.reshape(N_GC, N_GR, ROWS_DEV, F).transpose(1, 0, 2, 3).reshape(NODES, F)
    grad_hidden = column_sums.astype(jnp.bfloat16)
    grad_features = jnp.dot(grad_hidden, weight.T, preferred_element_type=jnp.float32).astype(jnp.bfloat16)
    grad_weight = jnp.dot(features.T, grad_hidden, preferred_element_type=jnp.float32) / math.sqrt(NODES)
    return (output, grad_features, grad_weight)
```

```python
import functools
import math

import jax
import jax.numpy as jnp
from jax import lax
from jax.experimental import pallas as pl
from jax.experimental.pallas import tpu as pltpu
from jax.sharding import PartitionSpec as P

TS = 128
F32 = jnp.float32
BF16 = jnp.bfloat16
LAG = 2
MIB = 2**20
VMEM_LIMIT = 8 * MIB

ORDER = (
    [(f, 2, t) for f in (1, 0) for t in (0, 1)]
    + [(f, 1, t) for f in (1, 0) for t in (2, 3)]
    + [(f, 2, t) for f in (1, 0) for t in (2, 3)]
    + [(f, 3, t) for f in (1, 0) for t in (0, 1)]
    + [(f, 1, t) for f in (1, 0) for t in (0, 1)]
    + [(f, 3, t) for f in (1, 0) for t in (2, 3)]
    + [(f, 0, t) for f in (1, 0) for t in range(4)]
)
ARRIVAL = [(f, r, t) for r in (0, 1, 3, 2) for f in (0, 1) for t in range(4)]


def places(order):
    at = [0] * 32
    for i, (far, ring, tile) in enumerate(order):
        at[far * 16 + ring * 4 + tile] = i
    return at


def look_up(index, entries):
    total = jnp.zeros_like(index)
    for at, value in enumerate(entries):
        total = jnp.where(index == at, value, total)
    return total


def group_plan(keys, others, live, cuts, pad, unroll, pad_tile):
    n = keys.shape[0]
    n_keys, n_phases = cuts[-1], len(cuts) - 1
    pad_bits, turn_bits = pad.bit_length() - 1, unroll.bit_length() - 1
    key = jnp.where(live, keys, n_keys)
    slot = jnp.arange(n, dtype=jnp.int32)
    before = (key[:, None] == key[None, :]) & (slot[None, :] < slot[:, None])
    rank = jnp.sum(before.astype(jnp.int32), axis=1)
    every = jnp.arange(n_keys, dtype=jnp.int32)
    counts = jnp.sum((key[None, :] == every[:, None]).astype(jnp.int32), axis=1)
    groups = (counts + pad - 1) >> pad_bits
    phase = jnp.zeros_like(every)
    for cut in cuts[1:-1]:
        phase = phase + (every >= cut).astype(jnp.int32)
    phases = jnp.arange(n_phases, dtype=jnp.int32)
    held = jnp.sum(jnp.where(phase[None, :] == phases[:, None], groups[None, :], 0), axis=1)
    turns = (held + unroll - 1) >> turn_bits
    edges = jnp.arange(n_phases + 1, dtype=jnp.int32)
    bounds = jnp.sum(jnp.where(phases[None, :] < edges[:, None], turns[None, :], 0), axis=1)
    earlier = jnp.where(phases[None, :] < phase[:, None], turns[None, :] << turn_bits, 0)
    ahead = (phase[None, :] == phase[:, None]) & (every[None, :] < every[:, None])
    starts = jnp.sum(jnp.where(ahead, groups[None, :], 0), axis=1) + jnp.sum(earlier, axis=1)
    first = jnp.sum(jnp.where(key[:, None] == every[None, :], starts[None, :], 0), axis=1)
    place = jnp.where(live, (first << pad_bits) + rank, -1)
    most = (n + (pad - 1) * n_keys) // pad + n_phases * (unroll - 1)
    most = -(-most // unroll) * unroll
    spot = jnp.arange(most * pad, dtype=jnp.int32)
    hit = place[None, :] == spot[:, None]
    code = jnp.sum(jnp.where(hit, ((slot << 7) + others - pad_tile)[None, :], 0), axis=1) + pad_tile
    turn = jnp.arange(most, dtype=jnp.int32)
    group_key = jnp.sum((starts[None, :] <= turn[:, None]).astype(jnp.int32), axis=1) - 1
    return bounds, code >> 7, code & 127, group_key


def group_kernel(
    table_cuts, table_size, phase, first_key, pad, unroll, forward, n_extra, finish, *refs
):
    bounds_ref, tile_ref, other_ref, key_ref, tiles_ref = refs[:5]
    n_tables = len(table_cuts)
    table_refs = refs[5 : 5 + n_tables]
    extra_refs = refs[5 + n_tables : 5 + n_tables + n_extra]
    out_refs = refs[5 + n_tables + n_extra : -2]
    table, acc = refs[-2:]
    for ref, (at, start, size) in zip(table_refs, table_cuts):
        table[at : at + size] = ref[start : start + size]
    table[table_size] = jnp.zeros((TS, TS), table.dtype)
    acc[...] = jnp.zeros_like(acc)

    def product(group):
        picked = [tiles_ref[tile_ref[group * pad + i]] for i in range(pad)]
        rest = [table[other_ref[group * pad + i]] for i in range(pad)]
        if forward:
            left, right = picked, rest
        else:
            left, right = rest, picked
        return jnp.dot(
            jnp.concatenate(left, 1), jnp.concatenate(right, 0), preferred_element_type=F32
        )

    @pl.loop(bounds_ref[phase], bounds_ref[phase + 1])
    def _(turn):
        waiting = []
        for i in range(unroll):
            waiting.append((key_ref[turn * unroll + i] - first_key, product(turn * unroll + i)))
            if len(waiting) > LAG:
                key, value = waiting.pop(0)
                acc[key] += value
        for key, value in waiting:
            acc[key] += value

    finish(acc, extra_refs, out_refs)


def group_pass(
    plan, tiles, tables, table_size, phase, keys, pad, unroll, forward, extras, outs, finish, name
):
    bounds, tile_at, other_at, key_at = plan
    scalar = pl.BlockSpec(memory_space=pltpu.SMEM)
    here = pl.BlockSpec(memory_space=pltpu.VMEM)
    n_keys = keys[1] - keys[0]
    share = tiles.shape[0] * n_keys // 64 if forward else tiles.shape[0] * n_keys // 96
    return pl.pallas_call(
        functools.partial(
            group_kernel,
            tuple(t[1:] for t in tables),
            table_size,
            phase,
            keys[0],
            pad,
            unroll,
            forward,
            len(extras),
            finish,
        ),
        out_shape=outs,
        in_specs=[scalar] * 4 + [here] * (1 + len(tables) + len(extras)),
        out_specs=[here] * len(outs),
        scratch_shapes=[
            pltpu.VMEM((table_size + 1, TS, TS), BF16),
            pltpu.VMEM((n_keys, TS, TS), F32),
        ],
        compiler_params=pltpu.CompilerParams(vmem_limit_bytes=VMEM_LIMIT),
        cost_estimate=pl.CostEstimate(
            flops=2 * share * TS**3 * 8, bytes_accessed=4 * MIB, transcendentals=0
        ),
        name=name,
    )(bounds, tile_at, other_at, key_at, tiles, *[t[0] for t in tables], *extras)


def array(tiles, dtype=BF16):
    return jax.ShapeDtypeStruct((tiles, TS, TS), dtype)


def write_parts(acc, extra_refs, out_refs):
    del extra_refs
    at = 0
    for ref in out_refs:
        size = ref.shape[0]
        ref[...] = acc[at : at + size].astype(ref.dtype)
        at += size


def finish_early(acc, extra_refs, out_refs):
    del extra_refs
    out_refs[0][...] = acc[...]


def finish_theirs(acc, extra_refs, out_refs):
    early, own, following, previous, opposite = extra_refs
    theirs, weight_part = out_refs
    theirs[0:32] = (acc[...] + early[...]).astype(BF16)
    across = own[8].astype(F32) + opposite[4].astype(F32)
    beside = following[8].astype(F32) + previous[8].astype(F32)
    total = (across + beside).astype(BF16)
    theirs[32] = total
    weight_part[0] = total


def finish_mine(acc, extra_refs, out_refs):
    (got,) = extra_refs
    plus2, minus2, keep_far, keep = out_refs
    plus2[0:4] = (acc[0:4] + got[16:20].astype(F32)).astype(BF16)
    plus2[4] = jnp.zeros((TS, TS), BF16)
    minus2[...] = (acc[4:8] + got[20:24].astype(F32)).astype(BF16)
    keep_far[...] = acc[8:12] + got[24:28].astype(F32)
    keep[...] = acc[12:16] + got[28:32].astype(F32)


def call(kernel, outs, name, tiles, *args):
    return pl.pallas_call(
        lambda tiles_ref, *refs: kernel(*refs),
        out_shape=outs,
        compiler_params=pltpu.CompilerParams(vmem_limit_bytes=VMEM_LIMIT),
        name=name,
    )(tiles, *args)


def gelu_pair(pre_act):
    coeff = 0.7978845608028654
    cubed = pre_act * pre_act * pre_act
    tanh_val = jnp.tanh(coeff * (pre_act + 0.044715 * cubed))
    gelu_value = 0.5 * pre_act * (1.0 + tanh_val)
    gelu_slope = 0.5 * (1.0 + tanh_val) + 0.5 * pre_act * (1.0 - tanh_val * tanh_val) * coeff * (
        1.0 + 3.0 * 0.044715 * pre_act * pre_act
    )
    return (gelu_value, gelu_slope)


def own_sum(keep, plus, minus, plus2, minus2, far, skip):
    at = 4 + skip + (0 if far else 2)
    to = 0 if far else 2
    first = keep[0:2].astype(F32) + minus[at : at + 2].astype(F32) + plus2[to : to + 2].astype(F32)
    second = keep[2:4].astype(F32) + plus[at : at + 2].astype(F32) + minus2[to : to + 2].astype(F32)
    return jnp.concatenate([first, second], 0)


def sums_kernel(keep_far, keep, plus, minus, plus2, minus2, out_ref):
    out_ref[0:4] = own_sum(keep, plus, minus, plus2, minus2, False, 0).astype(BF16)
    out_ref[4:8] = own_sum(keep_far, plus, minus, plus2, minus2, True, 0).astype(BF16)


def middle_kernel(mine, got, weight, cotangent, far_cotangent, out_ref, pair_ref):
    w = weight[...]
    terms = []
    for at, block_cotangent in ((0, cotangent), (4, far_cotangent)):
        sums = mine[at : at + 4].astype(F32) + got[4 - at : 8 - at].astype(F32)
        mixed = sums.reshape(4 * TS, TS)
        high = mixed.astype(BF16)
        low = (mixed - high.astype(F32)).astype(BF16)
        pre_act = jnp.dot(high, w, preferred_element_type=F32) + jnp.dot(
            low, w, preferred_element_type=F32
        )
        value, slope = gelu_pair(pre_act)
        if at == 0:
            out_ref[...] = value.astype(BF16)
        grad_pre = (block_cotangent[...].astype(F32) * slope).astype(BF16)
        for i in range(4):
            pair_ref[at + i] = lax.dot_general(
                w,
                grad_pre[i * TS : (i + 1) * TS],
                (((1,), (1,)), ((), ())),
                preferred_element_type=F32,
            ).astype(BF16)
        terms.append(
            lax.dot_general(
                high, grad_pre, (((0,), (0,)), ((), ())), preferred_element_type=F32
            )
        )
    pair_ref[8] = (terms[0] + terms[1]).astype(BF16)


def join_kernel(*refs):
    at = 0
    for ref in refs[:-1]:
        refs[-1][at : at + ref.shape[0]] = ref[...]
        at += ref.shape[0]


def add_core_kernel(mine, got, weight_part, plus, minus):
    weight_sum = (weight_part[0].astype(F32) + got[32].astype(F32)).astype(BF16)
    for at, ref in ((0, plus), (8, minus)):
        total = (mine[at : at + 8].astype(F32) + got[at : at + 8].astype(F32)).astype(BF16)
        ref[0:4] = total[0:4]
        ref[4] = weight_sum
        ref[5:9] = total[4:8]


def far_weight_kernel(keep, plus, minus, plus2, minus2, own_plus, out_ref):
    out_ref[0:4] = own_sum(keep, plus, minus, plus2, minus2, True, 1).astype(BF16)
    across = own_plus[4].astype(F32) + plus2[4].astype(F32)
    beside = plus[4].astype(F32) + minus[4].astype(F32)
    out_ref[4] = (across + beside).astype(BF16)


def last_kernel(scale, keep, plus, minus, plus2, minus2, own_far, got_far, grad_ref, weight_ref):
    total = own_sum(keep, plus, minus, plus2, minus2, False, 1) + got_far[0:4].astype(F32)
    for i in range(4):
        grad_ref[i * TS : (i + 1) * TS] = jnp.transpose(total[i]).astype(BF16)
    weight_ref[...] = (own_far[4].astype(F32) + got_far[4].astype(F32)) * scale


def ring_permutes(axis):
    if axis == "gr":
        up = [(i, (i + 4) % 16) for i in range(16)]
    else:
        up = [(i, (i & 4) | ((i + 1) & 3)) for i in range(8)]
    down = [(j, i) for i, j in up]
    return lambda v: lax.ppermute(v, axis, up), lambda v: lax.ppermute(v, axis, down)


def pair_permute(axis, mask):
    size = {"gr": 16, "gc": 8}[axis]
    return lambda value: lax.ppermute(value, axis, [(i, i ^ mask) for i in range(size)])


def local(features, weight, cotangent, tiles, tile_rows, tile_cols, tile_counts):
    gr, gc = lax.axis_index("gr"), lax.axis_index("gc")
    rows, cols = tile_rows[0, 0], tile_cols[0, 0]
    live = jnp.arange(rows.shape[0], dtype=jnp.int32) < tile_counts[0, 0]
    sent, arrived = places(ORDER), places(ARRIVAL)

    owner = rows >> 2
    row_at = (((owner ^ gc) >> 2) & 1) * 16 + ((owner - gc) & 3) * 4 + (rows & 3)
    row_sent, row_arrived = look_up(row_at, sent), look_up(row_at, arrived)
    holder = cols >> 2
    core = (holder ^ gr) & 1
    col_at = (((holder ^ gr) >> 1) & 1) * 16 + (((holder >> 2) - (gr >> 2)) & 3) * 4 + (cols & 3)
    col_sent, col_arrived = look_up(col_at, sent), look_up(col_at, arrived)
    forward_plan = group_plan(row_sent, core * 32 + col_arrived, live, (0, 16, 32), 4, 16, 64)
    theirs_key = jnp.where(row_arrived < 24, 0, 32) + col_sent
    back_key = jnp.where(core == 1, theirs_key, 64 + col_sent)
    backward_plan = group_plan(back_key, row_arrived, live, (0, 32, 64, 80, 96), 2, 16, 32)

    core_swap, y_swap = pair_permute("gr", 1), pair_permute("gr", 2)
    w_swap = pair_permute("gc", 4)
    z_up, z_down = ring_permutes("gr")
    x_up, x_down = ring_permutes("gc")

    own = features.reshape(4, TS, TS)
    far = y_swap(own)
    pair = jnp.concatenate([own, far], 0)
    previous, following = z_up(pair), z_down(pair)
    blocks = pltpu.with_memory_space_constraint(tiles[0, 0], pltpu.VMEM)
    held = call(join_kernel, array(8), "after_tiles", blocks, pair)
    near = call(join_kernel, array(24), "near_columns", blocks, held, following, previous)
    opposite = call(
        join_kernel, array(8), "opposite_columns",
        blocks, z_up(previous[:4]), z_down(following[4:8]),
    )
    tables = [
        (near, 0, 0, 24),
        (opposite, 24, 0, 8),
        (core_swap(near), 32, 0, 24),
        (core_swap(opposite), 56, 0, 8),
    ]
    plus, minus = group_pass(
        forward_plan, blocks, tables, 64, 0, (0, 16), 4, 16, True, [], [array(8)] * 2, write_parts,
        "forward_sent",
    )

    got_plus, got_minus = x_up(plus), x_down(minus)
    plus2, minus2, keep_far, keep = group_pass(
        forward_plan, blocks, tables, 64, 1, (16, 32), 4, 16, True, [],
        [array(4), array(4), array(4, F32), array(4, F32)], write_parts, "forward_kept",
    )
    got_plus2 = x_up((plus2.astype(F32) + got_plus[:4].astype(F32)).astype(BF16))
    got_minus2 = x_down((minus2.astype(F32) + got_minus[:4].astype(F32)).astype(BF16))
    got = (got_plus, got_minus, got_plus2, got_minus2)
    sums = call(sums_kernel, array(8), "row_sums", blocks, keep_far, keep, *got)
    output, pair = call(
        middle_kernel,
        [jax.ShapeDtypeStruct(cotangent.shape, BF16), array(9)],
        "middle",
        blocks, sums, w_swap(sums), weight, cotangent, w_swap(cotangent),
    )

    previous, following = x_up(pair), x_down(pair)
    opposite_near, opposite_far = x_up(previous[:4]), x_down(following[4:9])
    early = [(pair, 0, 0, 8), (following, 8, 0, 8), (previous, 16, 0, 8)]
    late = [(opposite_near, 24, 0, 4), (opposite_far, 28, 0, 4)]
    (sums,) = group_pass(
        backward_plan, blocks, early, 32, 0, (0, 32), 2, 16, False, [], [array(32, F32)],
        finish_early, "backward_early",
    )
    theirs, weight_part = group_pass(
        backward_plan, blocks, late, 32, 1, (32, 64), 2, 16, False,
        [sums, pair, following, previous, opposite_far], [array(33), array(1)],
        finish_theirs, "backward_theirs",
    )

    got = core_swap(theirs)
    (mine,) = group_pass(
        backward_plan, blocks, early + late, 32, 2, (64, 80), 2, 16, False, [], [array(16)],
        write_parts, "backward_sent",
    )
    plus, minus = call(add_core_kernel, [array(9)] * 2, "add_core", blocks, mine, got, weight_part)
    got_plus, got_minus = z_up(plus), z_down(minus)
    plus2, minus2, keep_far, keep = group_pass(
        backward_plan, blocks, early + late, 32, 3, (80, 96), 2, 16, False, [got],
        [array(5), array(4), array(4, F32), array(4, F32)], finish_mine, "backward_kept",
    )
    got_plus2 = z_up((plus2.astype(F32) + got_plus[:5].astype(F32)).astype(BF16))
    got_minus2 = z_down((minus2.astype(F32) + got_minus[:4].astype(F32)).astype(BF16))
    got = (got_plus, got_minus, got_plus2, got_minus2)
    far = call(far_weight_kernel, array(5), "far_columns", blocks, keep_far, *got, plus)
    nodes = features.shape[0] * lax.axis_size("gr") * lax.axis_size("gc")
    grad_features, grad_weight = call(
        functools.partial(last_kernel, 1.0 / math.sqrt(nodes)),
        [jax.ShapeDtypeStruct(features.shape, BF16), jax.ShapeDtypeStruct((TS, TS), F32)],
        "last",
        blocks, keep, *got, far, y_swap(far),
    )
    return (output, grad_features, grad_weight)


def solution(mesh):
    return jax.shard_map(
        local,
        mesh=mesh,
        in_specs=(
            P(("gr", "gc"), None),
            P(),
            P(("gr", "gc"), None),
            P("gr", "gc", None, None, None),
            P("gr", "gc", None),
            P("gr", "gc", None),
            P("gr", "gc"),
        ),
        out_specs=(P(("gr", "gc"), None), P(("gr", "gc"), None), P()),
        check_vma=False,
    )
```

```python
import functools
import math

import jax
import jax.numpy as jnp
from jax import lax
from jax.experimental import pallas as pl
from jax.experimental.pallas import tpu as pltpu
from jax.sharding import PartitionSpec as P

TS = 128
F32 = jnp.float32
BF16 = jnp.bfloat16
LAG = 2
MIB = 2**20
VMEM_LIMIT = 8 * MIB

ORDER = (
    [(f, 2, t) for f in (1, 0) for t in (0, 1)]
    + [(f, 1, t) for f in (1, 0) for t in (2, 3)]
    + [(f, 2, t) for f in (1, 0) for t in (2, 3)]
    + [(f, 3, t) for f in (1, 0) for t in (0, 1)]
    + [(f, 1, t) for f in (1, 0) for t in (0, 1)]
    + [(f, 3, t) for f in (1, 0) for t in (2, 3)]
    + [(f, 0, t) for f in (1, 0) for t in range(4)]
)
ARRIVAL = [(f, r, t) for r in (0, 1, 3, 2) for f in (0, 1) for t in range(4)]


def places(order):
    at = [0] * 32
    for i, (far, ring, tile) in enumerate(order):
        at[far * 16 + ring * 4 + tile] = i
    return at


def look_up(index, entries):
    total = jnp.zeros_like(index)
    for at, value in enumerate(entries):
        total = jnp.where(index == at, value, total)
    return total


def group_plan(keys, others, live, cuts, pad, unroll, pad_tile):
    n = keys.shape[0]
    n_keys, n_phases = cuts[-1], len(cuts) - 1
    pad_bits, turn_bits = pad.bit_length() - 1, unroll.bit_length() - 1
    key = jnp.where(live, keys, n_keys)
    slot = jnp.arange(n, dtype=jnp.int32)
    before = (key[:, None] == key[None, :]) & (slot[None, :] < slot[:, None])
    rank = jnp.sum(before.astype(jnp.int32), axis=1)
    every = jnp.arange(n_keys, dtype=jnp.int32)
    counts = jnp.sum((key[None, :] == every[:, None]).astype(jnp.int32), axis=1)
    groups = (counts + pad - 1) >> pad_bits
    phase = jnp.zeros_like(every)
    for cut in cuts[1:-1]:
        phase = phase + (every >= cut).astype(jnp.int32)
    phases = jnp.arange(n_phases, dtype=jnp.int32)
    held = jnp.sum(jnp.where(phase[None, :] == phases[:, None], groups[None, :], 0), axis=1)
    turns = (held + unroll - 1) >> turn_bits
    edges = jnp.arange(n_phases + 1, dtype=jnp.int32)
    bounds = jnp.sum(jnp.where(phases[None, :] < edges[:, None], turns[None, :], 0), axis=1)
    earlier = jnp.where(phases[None, :] < phase[:, None], turns[None, :] << turn_bits, 0)
    ahead = (phase[None, :] == phase[:, None]) & (every[None, :] < every[:, None])
    starts = jnp.sum(jnp.where(ahead, groups[None, :], 0), axis=1) + jnp.sum(earlier, axis=1)
    first = jnp.sum(jnp.where(key[:, None] == every[None, :], starts[None, :], 0), axis=1)
    place = jnp.where(live, (first << pad_bits) + rank, -1)
    most = (n + (pad - 1) * n_keys) // pad + n_phases * (unroll - 1)
    most = -(-most // unroll) * unroll
    spot = jnp.arange(most * pad, dtype=jnp.int32)
    hit = place[None, :] == spot[:, None]
    code = jnp.sum(jnp.where(hit, ((slot << 7) + others - pad_tile)[None, :], 0), axis=1) + pad_tile
    turn = jnp.arange(most, dtype=jnp.int32)
    group_key = jnp.sum((starts[None, :] <= turn[:, None]).astype(jnp.int32), axis=1) - 1
    return bounds, code >> 7, code & 127, group_key


def group_kernel(
    table_cuts, table_size, phase, first_key, pad, unroll, forward, n_extra, finish, *refs
):
    bounds_ref, tile_ref, other_ref, key_ref, tiles_ref = refs[:5]
    n_tables = len(table_cuts)
    table_refs = refs[5 : 5 + n_tables]
    extra_refs = refs[5 + n_tables : 5 + n_tables + n_extra]
    out_refs = refs[5 + n_tables + n_extra : -2]
    table, acc = refs[-2:]
    for ref, (at, start, size) in zip(table_refs, table_cuts):
        table[at : at + size] = ref[start : start + size]
    table[table_size] = jnp.zeros((TS, TS), table.dtype)
    acc[...] = jnp.zeros_like(acc)

    def product(group):
        picked = [tiles_ref[tile_ref[group * pad + i]] for i in range(pad)]
        rest = [table[other_ref[group * pad + i]] for i in range(pad)]
        if forward:
            left, right = picked, rest
        else:
            left, right = rest, picked
        return jnp.dot(
            jnp.concatenate(left, 1), jnp.concatenate(right, 0), preferred_element_type=F32
        )

    @pl.loop(bounds_ref[phase], bounds_ref[phase + 1])
    def _(turn):
        waiting = []
        for i in range(unroll):
            waiting.append((key_ref[turn * unroll + i] - first_key, product(turn * unroll + i)))
            if len(waiting) > LAG:
                key, value = waiting.pop(0)
                acc[key] += value
        for key, value in waiting:
            acc[key] += value

    finish(acc, extra_refs, out_refs)


def group_pass(
    plan, tiles, tables, table_size, phase, keys, pad, unroll, forward, extras, outs, finish, name
):
    bounds, tile_at, other_at, key_at = plan
    scalar = pl.BlockSpec(memory_space=pltpu.SMEM)
    here = pl.BlockSpec(memory_space=pltpu.VMEM)
    n_keys = keys[1] - keys[0]
    share = tiles.shape[0] * n_keys // 64 if forward else tiles.shape[0] * n_keys // 96
    return pl.pallas_call(
        functools.partial(
            group_kernel,
            tuple(t[1:] for t in tables),
            table_size,
            phase,
            keys[0],
            pad,
            unroll,
            forward,
            len(extras),
            finish,
        ),
        out_shape=outs,
        in_specs=[scalar] * 4 + [here] * (1 + len(tables) + len(extras)),
        out_specs=[here] * len(outs),
        scratch_shapes=[
            pltpu.VMEM((table_size + 1, TS, TS), BF16),
            pltpu.VMEM((n_keys, TS, TS), F32),
        ],
        compiler_params=pltpu.CompilerParams(vmem_limit_bytes=VMEM_LIMIT),
        cost_estimate=pl.CostEstimate(
            flops=2 * share * TS**3 * 8, bytes_accessed=4 * MIB, transcendentals=0
        ),
        name=name,
    )(bounds, tile_at, other_at, key_at, tiles, *[t[0] for t in tables], *extras)


def array(tiles, dtype=BF16):
    return jax.ShapeDtypeStruct((tiles, TS, TS), dtype)


def write_parts(acc, extra_refs, out_refs):
    del extra_refs
    at = 0
    for ref in out_refs:
        size = ref.shape[0]
        ref[...] = acc[at : at + size].astype(ref.dtype)
        at += size


def finish_parts(first, acc, extra_refs, out_refs):
    early = extra_refs[0]
    at = 0
    for ref in out_refs:
        size = ref.shape[0]
        total = acc[at : at + size] + early[first + at : first + at + size]
        ref[...] = total.astype(ref.dtype)
        at += size


def finish_near(acc, extra_refs, out_refs):
    out_refs[0][...] = acc[...]
    out_refs[1][...] = extra_refs[0][...]


def finish_early(acc, extra_refs, out_refs):
    del extra_refs
    out_refs[0][...] = acc[...]


def finish_theirs(acc, extra_refs, out_refs):
    early, own, following, previous, opposite = extra_refs
    theirs, weight_part = out_refs
    theirs[0:32] = (acc[...] + early[...]).astype(BF16)
    across = own[8].astype(F32) + opposite[4].astype(F32)
    beside = following[8].astype(F32) + previous[8].astype(F32)
    total = (across + beside).astype(BF16)
    theirs[32] = total
    weight_part[0] = total


def finish_mine(acc, extra_refs, out_refs):
    (got,) = extra_refs
    plus2, minus2, keep_far, keep = out_refs
    plus2[0:4] = (acc[0:4] + got[16:20].astype(F32)).astype(BF16)
    plus2[4] = jnp.zeros((TS, TS), BF16)
    minus2[...] = (acc[4:8] + got[20:24].astype(F32)).astype(BF16)
    keep_far[...] = acc[8:12] + got[24:28].astype(F32)
    keep[...] = acc[12:16] + got[28:32].astype(F32)


def call(kernel, outs, name, tiles, *args):
    return pl.pallas_call(
        lambda tiles_ref, *refs: kernel(*refs),
        out_shape=outs,
        compiler_params=pltpu.CompilerParams(vmem_limit_bytes=VMEM_LIMIT),
        name=name,
    )(tiles, *args)


def gelu_pair(pre_act):
    coeff = 0.7978845608028654
    cubed = pre_act * pre_act * pre_act
    tanh_val = jnp.tanh(coeff * (pre_act + 0.044715 * cubed))
    gelu_value = 0.5 * pre_act * (1.0 + tanh_val)
    gelu_slope = 0.5 * (1.0 + tanh_val) + 0.5 * pre_act * (1.0 - tanh_val * tanh_val) * coeff * (
        1.0 + 3.0 * 0.044715 * pre_act * pre_act
    )
    return (gelu_value, gelu_slope)


def own_sum(keep, plus, minus, plus2, minus2, far, skip):
    at = 4 + skip + (0 if far else 2)
    to = 0 if far else 2
    first = keep[0:2].astype(F32) + minus[at : at + 2].astype(F32) + plus2[to : to + 2].astype(F32)
    second = keep[2:4].astype(F32) + plus[at : at + 2].astype(F32) + minus2[to : to + 2].astype(F32)
    return jnp.concatenate([first, second], 0)


def sums_kernel(
    keep_far, keep, plus, minus, plus2, minus2, rows, cols, out_ref, rows_out, cols_out
):
    rows_out[...] = rows[...]
    cols_out[...] = cols[...]
    out_ref[0:4] = own_sum(keep, plus, minus, plus2, minus2, False, 0).astype(BF16)
    out_ref[4:8] = own_sum(keep_far, plus, minus, plus2, minus2, True, 0).astype(BF16)


def middle_kernel(mine, got, weight, cotangent, far_cotangent, out_ref, pair_ref):
    w = weight[...]
    terms = []
    for at, block_cotangent in ((0, cotangent), (4, far_cotangent)):
        sums = mine[at : at + 4].astype(F32) + got[4 - at : 8 - at].astype(F32)
        mixed = sums.reshape(4 * TS, TS)
        high = mixed.astype(BF16)
        low = (mixed - high.astype(F32)).astype(BF16)
        pre_act = jnp.dot(high, w, preferred_element_type=F32) + jnp.dot(
            low, w, preferred_element_type=F32
        )
        value, slope = gelu_pair(pre_act)
        if at == 0:
            out_ref[...] = value.astype(BF16)
        grad_pre = (block_cotangent[...].reshape(4 * TS, TS).astype(F32) * slope).astype(BF16)
        for i in range(4):
            pair_ref[at + i] = lax.dot_general(
                w,
                grad_pre[i * TS : (i + 1) * TS],
                (((1,), (1,)), ((), ())),
                preferred_element_type=F32,
            ).astype(BF16)
        terms.append(
            lax.dot_general(
                high, grad_pre, (((0,), (0,)), ((), ())), preferred_element_type=F32
            )
        )
    pair_ref[8] = (terms[0] + terms[1]).astype(BF16)


def near_kernel(own, following, previous, near_out, first_out, second_out):
    near_out[0:8] = own[...]
    near_out[8:16] = following[...]
    near_out[16:24] = previous[...]
    first_out[...] = previous[0:4]
    second_out[...] = following[4:8]


def columns_kernel(near, first, second, cotangent, out_ref, cotangent_out):
    out_ref[0:24] = near[...]
    out_ref[24:28] = first[...]
    out_ref[28:32] = second[...]
    cotangent_out[...] = cotangent[...]


def join(name, *parts):
    return pl.pallas_call(
        join_kernel,
        out_shape=array(sum(p.shape[0] for p in parts)),
        compiler_params=pltpu.CompilerParams(vmem_limit_bytes=VMEM_LIMIT),
        name=name,
    )(*parts)


def join_kernel(*refs):
    at = 0
    for ref in refs[:-1]:
        refs[-1][at : at + ref.shape[0]] = ref[...]
        at += ref.shape[0]


def add_core_kernel(mine, got, weight_part, plus, minus):
    weight_sum = (weight_part[0].astype(F32) + got[32].astype(F32)).astype(BF16)
    for at, ref in ((0, plus), (8, minus)):
        total = (mine[at : at + 8].astype(F32) + got[at : at + 8].astype(F32)).astype(BF16)
        ref[0:4] = total[0:4]
        ref[4] = weight_sum
        ref[5:9] = total[4:8]


def far_weight_kernel(keep, plus, minus, plus2, minus2, own_plus, out_ref):
    out_ref[0:4] = own_sum(keep, plus, minus, plus2, minus2, True, 1).astype(BF16)
    across = own_plus[4].astype(F32) + plus2[4].astype(F32)
    beside = plus[4].astype(F32) + minus[4].astype(F32)
    out_ref[4] = (across + beside).astype(BF16)


def last_kernel(scale, keep, plus, minus, plus2, minus2, own_far, got_far, grad_ref, weight_ref):
    total = own_sum(keep, plus, minus, plus2, minus2, False, 1) + got_far[0:4].astype(F32)
    for i in range(4):
        grad_ref[i * TS : (i + 1) * TS] = jnp.transpose(total[i]).astype(BF16)
    weight_ref[...] = (own_far[4].astype(F32) + got_far[4].astype(F32)) * scale


def ring_permutes(axis):
    if axis == "gr":
        up = [(i, (i + 4) % 16) for i in range(16)]
    else:
        up = [(i, (i & 4) | ((i + 1) & 3)) for i in range(8)]
    down = [(j, i) for i, j in up]
    return lambda v: lax.ppermute(v, axis, up), lambda v: lax.ppermute(v, axis, down)


def pair_permute(axis, mask):
    size = {"gr": 16, "gc": 8}[axis]
    return lambda value: lax.ppermute(value, axis, [(i, i ^ mask) for i in range(size)])


def local(features, weight, cotangent, tiles, tile_rows, tile_cols, tile_counts):
    gr, gc = lax.axis_index("gr"), lax.axis_index("gc")
    rows, cols = tile_rows[0, 0], tile_cols[0, 0]
    live = jnp.arange(rows.shape[0], dtype=jnp.int32) < tile_counts[0, 0]
    sent, arrived = places(ORDER), places(ARRIVAL)

    owner = rows >> 2
    row_at = (((owner ^ gc) >> 2) & 1) * 16 + ((owner - gc) & 3) * 4 + (rows & 3)
    row_sent = look_up(row_at, sent)
    holder = cols >> 2
    core = (holder ^ gr) & 1
    col_at = (((holder ^ gr) >> 1) & 1) * 16 + (((holder >> 2) - (gr >> 2)) & 3) * 4 + (cols & 3)
    col_arrived = look_up(col_at, arrived)
    near_own = (core == 0) & (col_arrived < 24)
    forward_key = jnp.where(near_own, 0, 32) + row_sent
    forward_plan = group_plan(
        forward_key, core * 32 + col_arrived, live, (0, 32, 48, 64), 2, 32, 64
    )
    core_swap, y_swap = pair_permute("gr", 1), pair_permute("gr", 2)
    w_swap = pair_permute("gc", 4)
    z_up, z_down = ring_permutes("gr")
    x_up, x_down = ring_permutes("gc")

    own = features.reshape(4, TS, TS)
    pair = jnp.concatenate([own, y_swap(own)], 0)
    previous, following = z_up(pair), z_down(pair)
    blocks = pltpu.with_memory_space_constraint(tiles[0, 0], pltpu.VMEM)
    held = call(join_kernel, array(8), "after_tiles", blocks, pair)
    near, first, second = call(
        near_kernel, [array(24), array(4), array(4)], "near_columns",
        blocks, held, following, previous,
    )
    opposite_near, opposite_far = z_up(first), z_down(second)
    early, near = group_pass(
        forward_plan, blocks, [(near, 0, 0, 24)], 64, 0, (0, 32), 2, 32, True, [near],
        [array(32, F32), array(24)], finish_near, "forward_early",
    )
    columns, own_cotangent = call(
        columns_kernel, [array(32), array(4)], "own_columns",
        blocks, near, opposite_near, opposite_far, cotangent.reshape(4, TS, TS),
    )
    tables = [(columns, 0, 0, 32), (core_swap(columns), 32, 0, 32)]
    far_cotangent = w_swap(own_cotangent)
    plus, minus = group_pass(
        forward_plan, blocks, tables, 64, 1, (32, 48), 2, 32, True, [early],
        [array(8)] * 2, functools.partial(finish_parts, 0), "forward_sent",
    )

    got_plus, got_minus = x_up(plus), x_down(minus)
    plus2, minus2, keep_far, keep = group_pass(
        forward_plan, blocks, tables, 64, 2, (48, 64), 2, 32, True, [early, far_cotangent],
        [array(4), array(4), array(4, F32), array(4, F32)], functools.partial(finish_parts, 16),
        "forward_kept",
    )
    got_plus2 = x_up((plus2.astype(F32) + got_plus[:4].astype(F32)).astype(BF16))
    got_minus2 = x_down((minus2.astype(F32) + got_minus[:4].astype(F32)).astype(BF16))
    got = (got_plus, got_minus, got_plus2, got_minus2)
    sums, later_rows, later_cols = call(
        sums_kernel, [array(8), row_at, col_at], "row_sums",
        blocks, keep_far, keep, *got, row_at, col_at,
    )
    row_arrived, col_sent = look_up(later_rows, arrived), look_up(later_cols, sent)
    theirs_key = jnp.where(row_arrived < 24, 0, 32) + col_sent
    back_key = jnp.where(core == 1, theirs_key, 64 + col_sent)
    backward_plan = group_plan(back_key, row_arrived, live, (0, 32, 64, 80, 96), 2, 32, 32)

    output, pair = call(
        middle_kernel,
        [jax.ShapeDtypeStruct(cotangent.shape, BF16), array(9)],
        "middle",
        blocks, sums, w_swap(sums), weight, cotangent, far_cotangent,
    )

    previous, following = x_up(pair), x_down(pair)
    opposite_near, opposite_far = x_up(previous[:4]), x_down(following[4:9])
    early = [(pair, 0, 0, 8), (following, 8, 0, 8), (previous, 16, 0, 8)]
    late = [(opposite_near, 24, 0, 4), (opposite_far, 28, 0, 4)]
    (sums,) = group_pass(
        backward_plan, blocks, early, 32, 0, (0, 32), 2, 32, False, [], [array(32, F32)],
        finish_early, "backward_early",
    )
    theirs, weight_part = group_pass(
        backward_plan, blocks, late, 32, 1, (32, 64), 2, 32, False,
        [sums, pair, following, previous, opposite_far], [array(33), array(1)],
        finish_theirs, "backward_theirs",
    )

    got = core_swap(theirs)
    (mine,) = group_pass(
        backward_plan, blocks, early + late, 32, 2, (64, 80), 2, 32, False, [], [array(16)],
        write_parts, "backward_sent",
    )
    plus, minus = call(add_core_kernel, [array(9)] * 2, "add_core", blocks, mine, got, weight_part)
    got_plus, got_minus = z_up(plus), z_down(minus)
    plus2, minus2, keep_far, keep = group_pass(
        backward_plan, blocks, early + late, 32, 3, (80, 96), 2, 32, False, [got],
        [array(5), array(4), array(4, F32), array(4, F32)], finish_mine, "backward_kept",
    )
    got_plus2 = z_up((plus2.astype(F32) + got_plus[:5].astype(F32)).astype(BF16))
    got_minus2 = z_down((minus2.astype(F32) + got_minus[:4].astype(F32)).astype(BF16))
    got = (got_plus, got_minus, got_plus2, got_minus2)
    far = call(far_weight_kernel, array(5), "far_columns", blocks, keep_far, *got, plus)
    nodes = features.shape[0] * lax.axis_size("gr") * lax.axis_size("gc")
    grad_features, grad_weight = call(
        functools.partial(last_kernel, 1.0 / math.sqrt(nodes)),
        [jax.ShapeDtypeStruct(features.shape, BF16), jax.ShapeDtypeStruct((TS, TS), F32)],
        "last",
        blocks, keep, *got, far, y_swap(far),
    )
    return (output, grad_features, grad_weight)


def solution(mesh):
    return jax.shard_map(
        local,
        mesh=mesh,
        in_specs=(
            P(("gr", "gc"), None),
            P(),
            P(("gr", "gc"), None),
            P("gr", "gc", None, None, None),
            P("gr", "gc", None),
            P("gr", "gc", None),
            P("gr", "gc"),
        ),
        out_specs=(P(("gr", "gc"), None), P(("gr", "gc"), None), P()),
        check_vma=False,
    )
```

```python
import functools
import math

import jax
import jax.numpy as jnp
from jax import lax
from jax.experimental import pallas as pl
from jax.experimental.pallas import tpu as pltpu
from jax.sharding import PartitionSpec as P

TS = 128
F32 = jnp.float32
BF16 = jnp.bfloat16
LAG = 2
MIB = 2**20
VMEM_LIMIT = 8 * MIB

ORDER = (
    [(f, 2, t) for f in (1, 0) for t in (0, 1)]
    + [(f, 1, t) for f in (1, 0) for t in (2, 3)]
    + [(f, 2, t) for f in (1, 0) for t in (2, 3)]
    + [(f, 3, t) for f in (1, 0) for t in (0, 1)]
    + [(f, 1, t) for f in (1, 0) for t in (0, 1)]
    + [(f, 3, t) for f in (1, 0) for t in (2, 3)]
    + [(f, 0, t) for f in (1, 0) for t in range(4)]
)
ARRIVAL = [(f, r, t) for r in (0, 1, 3, 2) for f in (0, 1) for t in range(4)]


def places(order):
    at = [0] * 32
    for i, (far, ring, tile) in enumerate(order):
        at[far * 16 + ring * 4 + tile] = i
    return at


def look_up(index, entries):
    total = jnp.zeros_like(index)
    for at, value in enumerate(entries):
        total = jnp.where(index == at, value, total)
    return total


def group_plan(keys, others, live, cuts, pad, unroll, pad_tile):
    n = keys.shape[0]
    n_keys, n_phases = cuts[-1], len(cuts) - 1
    pad_bits, turn_bits = pad.bit_length() - 1, unroll.bit_length() - 1
    key = jnp.where(live, keys, n_keys)
    slot = jnp.arange(n, dtype=jnp.int32)
    before = (key[:, None] == key[None, :]) & (slot[None, :] < slot[:, None])
    rank = jnp.sum(before.astype(jnp.int32), axis=1)
    every = jnp.arange(n_keys, dtype=jnp.int32)
    counts = jnp.sum((key[None, :] == every[:, None]).astype(jnp.int32), axis=1)
    groups = (counts + pad - 1) >> pad_bits
    phase = jnp.zeros_like(every)
    for cut in cuts[1:-1]:
        phase = phase + (every >= cut).astype(jnp.int32)
    phases = jnp.arange(n_phases, dtype=jnp.int32)
    held = jnp.sum(jnp.where(phase[None, :] == phases[:, None], groups[None, :], 0), axis=1)
    turns = (held + unroll - 1) >> turn_bits
    edges = jnp.arange(n_phases + 1, dtype=jnp.int32)
    bounds = jnp.sum(jnp.where(phases[None, :] < edges[:, None], turns[None, :], 0), axis=1)
    earlier = jnp.where(phases[None, :] < phase[:, None], turns[None, :] << turn_bits, 0)
    ahead = (phase[None, :] == phase[:, None]) & (every[None, :] < every[:, None])
    starts = jnp.sum(jnp.where(ahead, groups[None, :], 0), axis=1) + jnp.sum(earlier, axis=1)
    first = jnp.sum(jnp.where(key[:, None] == every[None, :], starts[None, :], 0), axis=1)
    place = jnp.where(live, (first << pad_bits) + rank, -1)
    most = (n + (pad - 1) * n_keys) // pad + n_phases * (unroll - 1)
    most = -(-most // unroll) * unroll
    spot = jnp.arange(most * pad, dtype=jnp.int32)
    hit = place[None, :] == spot[:, None]
    code = jnp.sum(jnp.where(hit, ((slot << 7) + others - pad_tile)[None, :], 0), axis=1) + pad_tile
    turn = jnp.arange(most, dtype=jnp.int32)
    group_key = jnp.sum((starts[None, :] <= turn[:, None]).astype(jnp.int32), axis=1) - 1
    return bounds, code >> 7, code & 127, group_key


def group_kernel(
    table_cuts, table_size, phase, first_key, pad, unroll, forward, n_extra, finish, *refs
):
    plan_refs, tiles_ref = refs[:4], refs[4]
    n_tables = len(table_cuts)
    table_refs = refs[5 : 5 + n_tables]
    extra_refs = refs[5 + n_tables : 5 + n_tables + n_extra]
    out_refs = refs[5 + n_tables + n_extra : -7]
    table, acc, bounds_ref, tile_ref, other_ref, key_ref, sems = refs[-7:]
    copies = [
        pltpu.make_async_copy(ref, here, sems.at[i])
        for i, (ref, here) in enumerate(zip(plan_refs, (bounds_ref, tile_ref, other_ref, key_ref)))
    ]
    for copy in copies:
        copy.start()
    for ref, (at, start, size) in zip(table_refs, table_cuts):
        table[at : at + size] = ref[start : start + size]
    table[table_size] = jnp.zeros((TS, TS), table.dtype)
    acc[...] = jnp.zeros_like(acc)
    for copy in copies:
        copy.wait()

    def product(group):
        picked = [tiles_ref[tile_ref[group * pad + i]] for i in range(pad)]
        rest = [table[other_ref[group * pad + i]] for i in range(pad)]
        if forward:
            left, right = picked, rest
        else:
            left, right = rest, picked
        return jnp.dot(
            jnp.concatenate(left, 1), jnp.concatenate(right, 0), preferred_element_type=F32
        )

    @pl.loop(bounds_ref[phase], bounds_ref[phase + 1])
    def _(turn):
        waiting = []
        for i in range(unroll):
            waiting.append((key_ref[turn * unroll + i] - first_key, product(turn * unroll + i)))
            if len(waiting) > LAG:
                key, value = waiting.pop(0)
                acc[key] += value
        for key, value in waiting:
            acc[key] += value

    finish(acc, extra_refs, out_refs)


def group_pass(
    plan, tiles, tables, table_size, phase, keys, pad, unroll, forward, extras, outs, finish, name
):
    bounds, tile_at, other_at, key_at = plan
    anywhere = pl.BlockSpec(memory_space=pl.ANY)
    here = pl.BlockSpec(memory_space=pltpu.VMEM)
    n_keys = keys[1] - keys[0]
    share = tiles.shape[0] * n_keys // 64 if forward else tiles.shape[0] * n_keys // 96
    return pl.pallas_call(
        functools.partial(
            group_kernel,
            tuple(t[1:] for t in tables),
            table_size,
            phase,
            keys[0],
            pad,
            unroll,
            forward,
            len(extras),
            finish,
        ),
        out_shape=outs,
        in_specs=[anywhere] * 4 + [here] * (1 + len(tables) + len(extras)),
        out_specs=[here] * len(outs),
        scratch_shapes=[
            pltpu.VMEM((table_size + 1, TS, TS), BF16),
            pltpu.VMEM((n_keys, TS, TS), F32),
            *[pltpu.SMEM(part.shape, part.dtype) for part in plan],
            pltpu.SemaphoreType.DMA((4,)),
        ],
        compiler_params=pltpu.CompilerParams(vmem_limit_bytes=VMEM_LIMIT),
        cost_estimate=pl.CostEstimate(
            flops=2 * share * TS**3 * 8, bytes_accessed=4 * MIB, transcendentals=0
        ),
        name=name,
    )(bounds, tile_at, other_at, key_at, tiles, *[t[0] for t in tables], *extras)


def array(tiles, dtype=BF16):
    return jax.ShapeDtypeStruct((tiles, TS, TS), dtype)


def write_parts(acc, extra_refs, out_refs):
    del extra_refs
    at = 0
    for ref in out_refs:
        size = ref.shape[0]
        ref[...] = acc[at : at + size].astype(ref.dtype)
        at += size


def finish_parts(first, acc, extra_refs, out_refs):
    early = extra_refs[0]
    at = 0
    for ref in out_refs:
        size = ref.shape[0]
        total = acc[at : at + size] + early[first + at : first + at + size]
        ref[...] = total.astype(ref.dtype)
        at += size


def finish_near(acc, extra_refs, out_refs):
    out_refs[0][...] = acc[...]
    out_refs[1][...] = extra_refs[0][...]


def finish_early(acc, extra_refs, out_refs):
    del extra_refs
    out_refs[0][...] = acc[...]


def finish_theirs(acc, extra_refs, out_refs):
    early, own, following, previous, opposite = extra_refs
    theirs, weight_part = out_refs
    theirs[0:32] = (acc[...] + early[...]).astype(BF16)
    across = own[8].astype(F32) + opposite[4].astype(F32)
    beside = following[8].astype(F32) + previous[8].astype(F32)
    total = (across + beside).astype(BF16)
    theirs[32] = total
    weight_part[0] = total


def finish_mine(acc, extra_refs, out_refs):
    (got,) = extra_refs
    plus2, minus2, keep_far, keep = out_refs
    plus2[0:4] = (acc[0:4] + got[16:20].astype(F32)).astype(BF16)
    plus2[4] = jnp.zeros((TS, TS), BF16)
    minus2[...] = (acc[4:8] + got[20:24].astype(F32)).astype(BF16)
    keep_far[...] = acc[8:12] + got[24:28].astype(F32)
    keep[...] = acc[12:16] + got[28:32].astype(F32)


def call(kernel, outs, name, tiles, *args):
    return pl.pallas_call(
        lambda tiles_ref, *refs: kernel(*refs),
        out_shape=outs,
        compiler_params=pltpu.CompilerParams(vmem_limit_bytes=VMEM_LIMIT),
        name=name,
    )(tiles, *args)


def gelu_pair(pre_act):
    coeff = 0.7978845608028654
    cubed = pre_act * pre_act * pre_act
    tanh_val = jnp.tanh(coeff * (pre_act + 0.044715 * cubed))
    gelu_value = 0.5 * pre_act * (1.0 + tanh_val)
    gelu_slope = 0.5 * (1.0 + tanh_val) + 0.5 * pre_act * (1.0 - tanh_val * tanh_val) * coeff * (
        1.0 + 3.0 * 0.044715 * pre_act * pre_act
    )
    return (gelu_value, gelu_slope)


def own_sum(keep, plus, minus, plus2, minus2, far, skip):
    at = 4 + skip + (0 if far else 2)
    to = 0 if far else 2
    first = keep[0:2].astype(F32) + minus[at : at + 2].astype(F32) + plus2[to : to + 2].astype(F32)
    second = keep[2:4].astype(F32) + plus[at : at + 2].astype(F32) + minus2[to : to + 2].astype(F32)
    return jnp.concatenate([first, second], 0)


def sums_kernel(
    keep_far, keep, plus, minus, plus2, minus2, rows, cols, out_ref, rows_out, cols_out
):
    rows_out[...] = rows[...]
    cols_out[...] = cols[...]
    out_ref[0:4] = own_sum(keep, plus, minus, plus2, minus2, False, 0).astype(BF16)
    out_ref[4:8] = own_sum(keep_far, plus, minus, plus2, minus2, True, 0).astype(BF16)


def middle_kernel(mine, got, weight, cotangent, far_cotangent, out_ref, pair_ref):
    w = weight[...]
    terms = []
    for at, block_cotangent in ((0, cotangent), (4, far_cotangent)):
        sums = mine[at : at + 4].astype(F32) + got[4 - at : 8 - at].astype(F32)
        mixed = sums.reshape(4 * TS, TS)
        high = mixed.astype(BF16)
        low = (mixed - high.astype(F32)).astype(BF16)
        pre_act = jnp.dot(high, w, preferred_element_type=F32) + jnp.dot(
            low, w, preferred_element_type=F32
        )
        value, slope = gelu_pair(pre_act)
        if at == 0:
            out_ref[...] = value.astype(BF16)
        grad_pre = (block_cotangent[...].reshape(4 * TS, TS).astype(F32) * slope).astype(BF16)
        for i in range(4):
            pair_ref[at + i] = lax.dot_general(
                w,
                grad_pre[i * TS : (i + 1) * TS],
                (((1,), (1,)), ((), ())),
                preferred_element_type=F32,
            ).astype(BF16)
        terms.append(
            lax.dot_general(
                high, grad_pre, (((0,), (0,)), ((), ())), preferred_element_type=F32
            )
        )
    pair_ref[8] = (terms[0] + terms[1]).astype(BF16)


def near_kernel(own, following, previous, near_out, first_out, second_out):
    near_out[0:8] = own[...]
    near_out[8:16] = following[...]
    near_out[16:24] = previous[...]
    first_out[...] = previous[0:4]
    second_out[...] = following[4:8]


def columns_kernel(near, first, second, cotangent, out_ref, cotangent_out):
    out_ref[0:24] = near[...]
    out_ref[24:28] = first[...]
    out_ref[28:32] = second[...]
    cotangent_out[...] = cotangent[...]


def join(name, *parts):
    return pl.pallas_call(
        join_kernel,
        out_shape=array(sum(p.shape[0] for p in parts)),
        compiler_params=pltpu.CompilerParams(vmem_limit_bytes=VMEM_LIMIT),
        name=name,
    )(*parts)


def join_kernel(*refs):
    at = 0
    for ref in refs[:-1]:
        refs[-1][at : at + ref.shape[0]] = ref[...]
        at += ref.shape[0]


def add_core_kernel(mine, got, weight_part, plus, minus):
    weight_sum = (weight_part[0].astype(F32) + got[32].astype(F32)).astype(BF16)
    for at, ref in ((0, plus), (8, minus)):
        total = (mine[at : at + 8].astype(F32) + got[at : at + 8].astype(F32)).astype(BF16)
        ref[0:4] = total[0:4]
        ref[4] = weight_sum
        ref[5:9] = total[4:8]


def far_weight_kernel(keep, plus, minus, plus2, minus2, own_plus, out_ref):
    out_ref[0:4] = own_sum(keep, plus, minus, plus2, minus2, True, 1).astype(BF16)
    across = own_plus[4].astype(F32) + plus2[4].astype(F32)
    beside = plus[4].astype(F32) + minus[4].astype(F32)
    out_ref[4] = (across + beside).astype(BF16)


def last_kernel(scale, keep, plus, minus, plus2, minus2, own_far, got_far, grad_ref, weight_ref):
    total = own_sum(keep, plus, minus, plus2, minus2, False, 1) + got_far[0:4].astype(F32)
    for i in range(4):
        grad_ref[i * TS : (i + 1) * TS] = jnp.transpose(total[i]).astype(BF16)
    weight_ref[...] = (own_far[4].astype(F32) + got_far[4].astype(F32)) * scale


def ring_permutes(axis):
    if axis == "gr":
        up = [(i, (i + 4) % 16) for i in range(16)]
    else:
        up = [(i, (i & 4) | ((i + 1) & 3)) for i in range(8)]
    down = [(j, i) for i, j in up]
    return lambda v: lax.ppermute(v, axis, up), lambda v: lax.ppermute(v, axis, down)


def pair_permute(axis, mask):
    size = {"gr": 16, "gc": 8}[axis]
    return lambda value: lax.ppermute(value, axis, [(i, i ^ mask) for i in range(size)])


def local(features, weight, cotangent, tiles, tile_rows, tile_cols, tile_counts):
    gr, gc = lax.axis_index("gr"), lax.axis_index("gc")
    both = (tile_rows * 64 + tile_cols)[0, 0]
    rows, cols = both >> 6, both & 63
    live = jnp.arange(rows.shape[0], dtype=jnp.int32) < tile_counts[0, 0]
    sent, arrived = places(ORDER), places(ARRIVAL)

    owner = rows >> 2
    row_at = (((owner ^ gc) >> 2) & 1) * 16 + ((owner - gc) & 3) * 4 + (rows & 3)
    row_sent = look_up(row_at, sent)
    holder = cols >> 2
    core = (holder ^ gr) & 1
    col_at = (((holder ^ gr) >> 1) & 1) * 16 + (((holder >> 2) - (gr >> 2)) & 3) * 4 + (cols & 3)
    col_arrived = look_up(col_at, arrived)
    near_own = (core == 0) & (col_arrived < 24)
    forward_key = jnp.where(near_own, 0, 32) + row_sent
    forward_plan = group_plan(
        forward_key, core * 32 + col_arrived, live, (0, 32, 48, 64), 2, 32, 64
    )
    core_swap, y_swap = pair_permute("gr", 1), pair_permute("gr", 2)
    w_swap = pair_permute("gc", 4)
    z_up, z_down = ring_permutes("gr")
    x_up, x_down = ring_permutes("gc")

    own = features.reshape(4, TS, TS)
    far = y_swap(own)
    pair = jnp.concatenate([join("own_block", own), far], 0)
    previous, following = z_up(pair), z_down(pair)
    blocks = pltpu.with_memory_space_constraint(tiles[0, 0], pltpu.VMEM)
    held = call(join_kernel, array(8), "after_tiles", blocks, pair)
    near, first, second = call(
        near_kernel, [array(24), array(4), array(4)], "near_columns",
        blocks, held, following, previous,
    )
    opposite_near, opposite_far = z_up(first), z_down(second)
    early, near = group_pass(
        forward_plan, blocks, [(near, 0, 0, 24)], 64, 0, (0, 32), 2, 32, True, [near],
        [array(32, F32), array(24)], finish_near, "forward_early",
    )
    columns, own_cotangent = call(
        columns_kernel, [array(32), array(4)], "own_columns",
        blocks, near, opposite_near, opposite_far, cotangent.reshape(4, TS, TS),
    )
    tables = [(columns, 0, 0, 32), (core_swap(columns), 32, 0, 32)]
    far_cotangent = w_swap(own_cotangent)
    plus, minus = group_pass(
        forward_plan, blocks, tables, 64, 1, (32, 48), 2, 32, True, [early],
        [array(8)] * 2, functools.partial(finish_parts, 0), "forward_sent",
    )

    got_plus, got_minus = x_up(plus), x_down(minus)
    plus2, minus2, keep_far, keep = group_pass(
        forward_plan, blocks, tables, 64, 2, (48, 64), 2, 32, True, [early, far_cotangent],
        [array(4), array(4), array(4, F32), array(4, F32)], functools.partial(finish_parts, 16),
        "forward_kept",
    )
    got_plus2 = x_up((plus2.astype(F32) + got_plus[:4].astype(F32)).astype(BF16))
    got_minus2 = x_down((minus2.astype(F32) + got_minus[:4].astype(F32)).astype(BF16))
    got = (got_plus, got_minus, got_plus2, got_minus2)
    sums, later_rows, later_cols = call(
        sums_kernel, [array(8), row_at, col_at], "row_sums",
        blocks, keep_far, keep, *got, row_at, col_at,
    )
    row_arrived, col_sent = look_up(later_rows, arrived), look_up(later_cols, sent)
    theirs_key = jnp.where(row_arrived < 24, 0, 32) + col_sent
    back_key = jnp.where(core == 1, theirs_key, 64 + col_sent)
    backward_plan = group_plan(back_key, row_arrived, live, (0, 32, 64, 80, 96), 2, 32, 32)

    output, pair = call(
        middle_kernel,
        [jax.ShapeDtypeStruct(cotangent.shape, BF16), array(9)],
        "middle",
        blocks, sums, w_swap(sums), weight, cotangent, far_cotangent,
    )

    previous, following = x_up(pair), x_down(pair)
    opposite_near, opposite_far = x_up(previous[:4]), x_down(following[4:9])
    early = [(pair, 0, 0, 8), (following, 8, 0, 8), (previous, 16, 0, 8)]
    late = [(opposite_near, 24, 0, 4), (opposite_far, 28, 0, 4)]
    (sums,) = group_pass(
        backward_plan, blocks, early, 32, 0, (0, 32), 2, 32, False, [], [array(32, F32)],
        finish_early, "backward_early",
    )
    theirs, weight_part = group_pass(
        backward_plan, blocks, late, 32, 1, (32, 64), 2, 32, False,
        [sums, pair, following, previous, opposite_far], [array(33), array(1)],
        finish_theirs, "backward_theirs",
    )

    got = core_swap(theirs)
    (mine,) = group_pass(
        backward_plan, blocks, early + late, 32, 2, (64, 80), 2, 32, False, [], [array(16)],
        write_parts, "backward_sent",
    )
    plus, minus = call(add_core_kernel, [array(9)] * 2, "add_core", blocks, mine, got, weight_part)
    got_plus, got_minus = z_up(plus), z_down(minus)
    plus2, minus2, keep_far, keep = group_pass(
        backward_plan, blocks, early + late, 32, 3, (80, 96), 2, 32, False, [got],
        [array(5), array(4), array(4, F32), array(4, F32)], finish_mine, "backward_kept",
    )
    got_plus2 = z_up((plus2.astype(F32) + got_plus[:5].astype(F32)).astype(BF16))
    got_minus2 = z_down((minus2.astype(F32) + got_minus[:4].astype(F32)).astype(BF16))
    got = (got_plus, got_minus, got_plus2, got_minus2)
    far = call(far_weight_kernel, array(5), "far_columns", blocks, keep_far, *got, plus)
    nodes = features.shape[0] * lax.axis_size("gr") * lax.axis_size("gc")
    grad_features, grad_weight = call(
        functools.partial(last_kernel, 1.0 / math.sqrt(nodes)),
        [jax.ShapeDtypeStruct(features.shape, BF16), jax.ShapeDtypeStruct((TS, TS), F32)],
        "last",
        blocks, keep, *got, far, y_swap(far),
    )
    return (output, grad_features, grad_weight)


def solution(mesh):
    return jax.shard_map(
        local,
        mesh=mesh,
        in_specs=(
            P(("gr", "gc"), None),
            P(),
            P(("gr", "gc"), None),
            P("gr", "gc", None, None, None),
            P("gr", "gc", None),
            P("gr", "gc", None),
            P("gr", "gc"),
        ),
        out_specs=(P(("gr", "gc"), None), P(("gr", "gc"), None), P()),
        check_vma=False,
    )
```
